512 devices in a mesh: freq: 16 (over y, core), bl: 32 (over z, x).
Axes of the slice: x: 4, y: 8, z: 8, core: 2. Of those that a mesh axis runs over, the one named last changes fastest.
Arguments:
- visibilities: bfloat16 [2, 64, 2, 32768], P(None, 'freq', None, 'bl'), may hold values from -168 to 168
- predicted_sky: bfloat16 [6, 2, 64, 2, 32768], P(None, None, 'freq', None, 'bl'), may hold values from -2 to 2
- station_pairs: int32 [2, 32768], P(None, 'bl'), may hold values from 0 to 511, as said below
- start_gains: float32 [2, 6, 64, 512], P(None, None, 'freq'), may hold values from 0.1 to 1.9
- kernel_width: int32 [6], replicated, may hold values from 1 to 2
Outputs:
- gains: float32 [2, 6, 64, 512], P(None, None, 'freq')
The draws below stay inside these ranges and needn't reach their ends.
Inputs may be any that keep to these rules, and one draw needn't show every extreme that they name: `station_pairs`: the two stations of a baseline differ; every station is the first station of some baselines.
All inputs are finite; a program needn't handle non-finite values.
Results may differ from the reference program's by a relative error of at most 0.0003.
Values sent between devices are 32-bit elements; how exact they have to be, the bound alone decides.
A program may use at most 64 MiB of HBM per device.

```python
import jax
import jax.numpy as jnp
from jax import lax

STATION_COUNT = 512
DIRECTION_COUNT = 6
CH = 4
TIME_COUNT = 2
ITERS = 4
CHANNEL_COUNT = 64
BASELINE_COUNT = 32768


def shared_draw(key):
    shift_key, shuffle_key, model_key, key_true, noise_key = jax.random.split(key, 5)
    leading_station = jnp.arange(BASELINE_COUNT, dtype=jnp.int32) % STATION_COUNT
    gain_shifts = jax.random.randint(shift_key, (BASELINE_COUNT,), 1, STATION_COUNT, dtype=jnp.int32)
    second_station = (leading_station + gain_shifts) % STATION_COUNT
    shuffled_indices = jax.random.permutation(shuffle_key, BASELINE_COUNT)
    station_pairs = jnp.stack([leading_station[shuffled_indices], second_station[shuffled_indices]]).astype(jnp.int32)
    predicted_sky = 0.5 * jnp.clip(jax.random.normal(model_key, (DIRECTION_COUNT, 2, CHANNEL_COUNT, TIME_COUNT, BASELINE_COUNT), jnp.float32), -4.0, 4.0)
    true_gains = 1.0 + 0.3 * jnp.clip(jax.random.normal(key_true, (2, DIRECTION_COUNT, CHANNEL_COUNT, STATION_COUNT), jnp.float32), -4.0, 4.0)
    thermal_noise = 0.3 * jnp.clip(jax.random.normal(noise_key, (2, CHANNEL_COUNT, TIME_COUNT, BASELINE_COUNT), jnp.float32), -4.0, 4.0)

    def one_channel(chan_index):
        gain_chan = lax.dynamic_index_in_dim(true_gains, chan_index, 2, keepdims=False)
        sky_chan = lax.dynamic_index_in_dim(predicted_sky, chan_index, 2, keepdims=False)
        left_gain = gain_chan[:, :, station_pairs[0]][:, :, None, :]
        right_gain = gain_chan[:, :, station_pairs[1]][:, :, None, :]
        fwd_re = left_gain[0] * sky_chan[:, 0] - left_gain[1] * sky_chan[:, 1]
        fwd_im = left_gain[0] * sky_chan[:, 1] + left_gain[1] * sky_chan[:, 0]
        one_re = fwd_re * right_gain[0] + fwd_im * right_gain[1]
        one_im = fwd_im * right_gain[0] - fwd_re * right_gain[1]
        return jnp.stack([jnp.sum(one_re, axis=0), jnp.sum(one_im, axis=0)])
    clean = lax.map(one_channel, jnp.arange(CHANNEL_COUNT, dtype=jnp.int32))
    observed = jnp.moveaxis(clean, 0, 1) + thermal_noise
    return (station_pairs, predicted_sky, observed)


def draw_station_pairs(key, part):
    common = shared_draw(key)
    return common[0]


def draw_predicted_sky(key, part):
    common = shared_draw(key)
    return common[1].astype(jnp.bfloat16)


def draw_visibilities(key, part):
    common = shared_draw(key)
    return common[2].astype(jnp.bfloat16)


def set_ends(result, key, smallest, high):
    longest = result.shape.index(max(result.shape))
    spots = []
    for shift in (0, 1):
        where = [jax.random.randint(jax.random.fold_in(key, axis), (), 0, length) for axis, length in enumerate(result.shape)]
        where[longest] = (where[longest] + shift) % result.shape[longest]
        spots.append(tuple(where))
    return result.at[spots[0]].set(smallest).at[spots[1]].set(high)


def setup_inputs(seed: int = 0) -> dict:
    streams_of = jax.random.split(jax.random.key(seed), 6)
    return {
        "visibilities": draw_visibilities(jax.random.fold_in(streams_of[5], 71), 0),
        "predicted_sky": draw_predicted_sky(jax.random.fold_in(streams_of[5], 71), 0),
        "station_pairs": draw_station_pairs(jax.random.fold_in(streams_of[5], 71), 0),
        "start_gains": jnp.clip(1.0 + 0.18 * jax.random.normal(streams_of[3], (2, DIRECTION_COUNT, CHANNEL_COUNT, STATION_COUNT), jnp.float32), 0.1, 1.9),
        "kernel_width": set_ends(jax.random.randint(streams_of[4], (DIRECTION_COUNT,), max(1, CH // 4), CH // 2 + 1), jax.random.fold_in(streams_of[4], 1), max(1, CH // 4), (CH // 2 + 1) - 1).astype(jnp.int32),
    }


def station_terms(left_re, left_im, right_re, right_im, sky_re, sky_im, vis_re, vis_im, time_axis):
    fwd_re = left_re * sky_re - left_im * sky_im
    fwd_im = left_re * sky_im + left_im * sky_re
    bwd_re = right_re * sky_re + right_im * sky_im
    bwd_im = right_re * sky_im - right_im * sky_re
    one_re = fwd_re * right_re + fwd_im * right_im
    one_im = fwd_im * right_re - fwd_re * right_im
    res_re = vis_re - jnp.sum(one_re, axis=0) + one_re
    res_im = vis_im - jnp.sum(one_im, axis=0) + one_im
    first_stop_index = jnp.stack([
        jnp.sum(res_re * bwd_re + res_im * bwd_im, axis=time_axis),
        jnp.sum(res_im * bwd_re - res_re * bwd_im, axis=time_axis),
        jnp.sum(bwd_re * bwd_re + bwd_im * bwd_im, axis=time_axis)])
    trailing_stop_index = jnp.stack([
        jnp.sum(res_re * fwd_re + res_im * fwd_im, axis=time_axis),
        jnp.sum(res_re * fwd_im - res_im * fwd_re, axis=time_axis),
        jnp.sum(fwd_re * fwd_re + fwd_im * fwd_im, axis=time_axis)])
    return first_stop_index.astype(jnp.bfloat16), trailing_stop_index.astype(jnp.bfloat16)


def reference(visibilities, predicted_sky, station_pairs, start_gains, kernel_width):
    leading_station = station_pairs[0]
    second_station = station_pairs[1]
    regular_weight = TIME_COUNT * BASELINE_COUNT / STATION_COUNT
    positions = jnp.arange(CHANNEL_COUNT, dtype=jnp.int32)
    gain_shifts = positions[None, :] - positions[:, None]
    inside = jnp.abs(gain_shifts) <= CH
    spread = kernel_width.astype(jnp.float32)[:, None, None]
    distance = gain_shifts.astype(jnp.float32)[None]
    weights = jnp.where(inside[None], jnp.exp(-(distance * distance) / (2.0 * spread * spread)), 0.0)
    totals = jnp.sum(weights, axis=2)

    def channel_normals(inputs):
        chan_index, gain_chan = inputs
        vis_chan = lax.dynamic_index_in_dim(visibilities, chan_index, 1, keepdims=False).astype(jnp.float32)
        sky_chan = lax.dynamic_index_in_dim(predicted_sky, chan_index, 2, keepdims=False).astype(jnp.float32)
        left_gain = gain_chan[:, :, leading_station][:, :, None, :]
        right_gain = gain_chan[:, :, second_station][:, :, None, :]
        first_stop_index, trailing_stop_index = station_terms(left_gain[0], left_gain[1], right_gain[0], right_gain[1],
                                              sky_chan[:, 0], sky_chan[:, 1], vis_chan[0], vis_chan[1], 1)
        leading_rows = first_stop_index.astype(jnp.float32).reshape(3 * DIRECTION_COUNT, BASELINE_COUNT).T
        trailing_rows = trailing_stop_index.astype(jnp.float32).reshape(3 * DIRECTION_COUNT, BASELINE_COUNT).T
        summed = jax.ops.segment_sum(leading_rows, leading_station, num_segments=STATION_COUNT)
        summed = summed + jax.ops.segment_sum(trailing_rows, second_station, num_segments=STATION_COUNT)
        return summed.T.reshape(3, DIRECTION_COUNT, STATION_COUNT)

    gain_now = start_gains
    for sweep in range(ITERS):
        normals = lax.map(channel_normals, (jnp.arange(CHANNEL_COUNT, dtype=jnp.int32), jnp.moveaxis(gain_now, 2, 0)))
        normals = jnp.moveaxis(normals, 0, 2)
        solved = (normals[0:2] + regular_weight * gain_now) / (normals[2][None] + regular_weight)
        updated = 0.5 * (gain_now + solved)
        gain_now = jnp.einsum("doj,rdjs->rdos", weights, updated,
                              precision=lax.Precision.HIGHEST) / totals[None, :, :, None]
    return gain_now
```

```python
import functools

import jax
import jax.numpy as jnp
from jax import lax
from jax.experimental import pallas as pl
from jax.experimental.pallas import tpu as pltpu
from jax.sharding import PartitionSpec as P

ITERS = 4
DIRS = 6
CHANS = 4
TIMES = 2
STATIONS = 512
NZ, NX = 8, 4
LANE = 128
BLOCKS = STATIONS // LANE
MESH = pl.DeviceIdType.MESH
F32, BF16 = jnp.float32, jnp.bfloat16


def hops(kz, kx):
    return min(kz, NZ - kz) + min(kx, NX - kx)


STEPS = sorted(
    [(kz, kx) for kz in range(NZ) for kx in range(NX) if kz or kx], key=lambda k: -hops(*k)
)


def owner_of(z):
    return jnp.logical_and(z != 3, z != 7), jnp.minimum(jnp.where(z > 3, z - 1, z), DIRS - 1)


def wait_for(ref, sem):
    pltpu.make_async_copy(ref, ref, sem).wait()


def kernel(
    nf, rho, vis_ref, sky_ref, ids_ref, gains_ref, width_ref, out_ref,
    gbuf, glhs, gat, oht, oh, terms, snd, rbuf, halo, upd, wts,
    rs_send, rs_recv, ag_send, ag_recv, ex_send, ex_recv,
):
    blocal = ids_ref.shape[1]
    f, bl = lax.axis_index("freq"), lax.axis_index("bl")
    z, x = lax.div(bl, NX), lax.rem(bl, NX)
    own, mine = owner_of(z)
    not_own = jnp.logical_not(own)
    has_up, has_down = f < nf - 1, f > 0

    def peer(kz, kx):
        return lax.rem(z + kz, NZ), lax.rem(x + kx, NX)

    halo[...] = jnp.zeros_like(halo)

    barrier = pltpu.get_barrier_semaphore()
    for kz, kx in STEPS:
        tz, tx = peer(kz, kx)
        pl.semaphore_signal(barrier, inc=1, device_id=(f, tz * NX + tx), device_id_type=MESH)

    for step in (1, nf - 1):
        neighbour = lax.rem(f + step, nf)
        pl.semaphore_signal(barrier, inc=1, device_id=(neighbour, bl), device_id_type=MESH)

    sub = lax.broadcasted_iota(jnp.int32, (8, LANE), 0)
    top = sub < CHANS

    for d in range(DIRS):
        for b in range(BLOCKS):
            lanes = slice(b * LANE, (b + 1) * LANE)
            gbuf[d, b] = jnp.concatenate(
                [gains_ref[0, d, :, lanes], gains_ref[1, d, :, lanes]], axis=0
            )

    spread = jnp.full((8, LANE), width_ref[mine], jnp.int32).astype(F32)
    chan = jnp.bitwise_and(sub, CHANS - 1)
    taps = []
    for j in range(3 * CHANS):
        shift = j - CHANS - chan
        there = f * CHANS + (j - CHANS)
        inside = (jnp.abs(shift) <= CHANS) & (there >= 0) & (there < nf * CHANS)
        distance = shift.astype(F32)
        taps.append(
            jnp.where(inside, jnp.exp(-(distance * distance) / (2.0 * spread * spread)), 0.0)
        )
    total = functools.reduce(jnp.add, taps)
    for j in range(3 * CHANS):
        wts[j] = taps[j] / total

    def fill(i, _):
        for h in range(2):
            row = ids_ref[h : h + 1, pl.ds(pl.multiple_of(i * LANE, LANE), LANE)]
            at = pl.multiple_of(h * blocal + i * LANE, LANE)
            station = lax.broadcasted_iota(jnp.int32, (STATIONS, LANE), 0)
            oht[:, pl.ds(at, LANE)] = jnp.where(station == row, 1.0, 0.0).astype(BF16)
            column = jnp.transpose(jnp.broadcast_to(row, (LANE, LANE)))
            for b in range(BLOCKS):
                station = lax.broadcasted_iota(jnp.int32, (LANE, LANE), 1) + b * LANE
                oh[pl.ds(at, LANE), b * LANE : (b + 1) * LANE] = jnp.where(
                    station == column, 1.0, 0.0
                ).astype(BF16)
        return 0

    lax.fori_loop(0, blocal // LANE, fill, 0)

    pl.semaphore_wait(barrier, len(STEPS) + 2)

    def swap(tile):
        return pltpu.roll(tile, CHANS, 0)

    def parts_of(tile):
        other = swap(tile)
        return jnp.where(top, tile, other), jnp.where(top, other, tile)

    def fold(a, b):
        return jnp.where(top, a, b) + swap(jnp.where(top, b, a))

    def chunk(i, _):
        lanes = pl.ds(pl.multiple_of(i * LANE, LANE), LANE)
        after = pl.ds(pl.multiple_of(blocal + i * LANE, LANE), LANE)
        sum_re, sum_im = vis_ref[0, :, lanes], vis_ref[1, :, lanes]
        kept = []
        for d in range(DIRS):
            hi, lo = slice(8 * d, 8 * d + 8), slice(8 * (DIRS + d), 8 * (DIRS + d) + 8)
            l_re, l_im = parts_of(gat[hi, lanes] + gat[lo, lanes])
            r_re, r_im = parts_of(gat[hi, after] + gat[lo, after])
            m_re, m_im = sky_ref[2 * d, :, lanes], sky_ref[2 * d + 1, :, lanes]
            z_re = l_re * m_re - l_im * m_im
            z_im = l_re * m_im + l_im * m_re
            y_re = r_re * m_re + r_im * m_im
            y_im = r_re * m_im - r_im * m_re
            u_re = z_re * r_re + z_im * r_im
            u_im = z_im * r_re - z_re * r_im
            sum_re, sum_im = sum_re - u_re, sum_im - u_im
            kept.append((z_re, z_im, y_re, y_im, u_re, u_im))
        first, second, first_den, second_den = [], [], [], []
        for z_re, z_im, y_re, y_im, u_re, u_im in kept:
            res_re, res_im = sum_re + u_re, sum_im + u_im
            first.append(fold(res_re * y_re + res_im * y_im, res_im * y_re - res_re * y_im))
            second.append(fold(res_re * z_re + res_im * z_im, res_re * z_im - res_im * z_re))
            first_den.append(y_re * y_re + y_im * y_im)
            second_den.append(z_re * z_re + z_im * z_im)
        for d in range(0, DIRS, 2):
            first.append(fold(first_den[d], first_den[d + 1]))
            second.append(fold(second_den[d], second_den[d + 1]))
        pad = jnp.zeros((8, LANE), F32)
        terms[:, lanes] = jnp.concatenate([*first, pad], axis=0).astype(BF16)
        terms[:, after] = jnp.concatenate([*second, pad], axis=0).astype(BF16)
        return 0

    def row_of(ref, e):
        return jnp.where(
            top,
            jnp.broadcast_to(ref[e : e + 1, :], (8, LANE)),
            jnp.broadcast_to(ref[CHANS + e : CHANS + e + 1, :], (8, LANE)),
        )

    def smooth(ref, side):
        return functools.reduce(
            jnp.add, [wts[side * CHANS + e] * row_of(ref, e) for e in range(CHANS)]
        )

    def sweep(it, _):
        parity = lax.rem(it, 2)
        for b in range(BLOCKS):
            for d in range(0, DIRS, 2):
                value = jnp.concatenate([gbuf[d, b], gbuf[d + 1, b]], axis=0)
                high = value.astype(BF16)
                low = (value - high.astype(F32)).astype(BF16)
                lanes = slice(b * LANE, (b + 1) * LANE)
                glhs[8 * d : 8 * d + 16, lanes] = high
                glhs[8 * (DIRS + d) : 8 * (DIRS + d) + 16, lanes] = low
        gat[...] = jnp.dot(glhs[...], oht[...], preferred_element_type=F32)
        lax.fori_loop(0, blocal // LANE, chunk, 0)
        normals = jnp.dot(terms[...], oh[...], preferred_element_type=F32)
        for b in range(BLOCKS):
            lanes = slice(b * LANE, (b + 1) * LANE)
            for d in range(DIRS):
                snd[d, b, 0:8] = normals[8 * d : 8 * d + 8, lanes]
                den = 8 * DIRS + CHANS * d
                snd[d, b, 8:12] = normals[den : den + CHANS, lanes]

        for kz, kx in STEPS:
            tz, tx = peer(kz, kx)
            there, which = owner_of(tz)

            @pl.when(there)
            def _():
                pltpu.make_async_remote_copy(
                    src_ref=snd.at[which, tx, pl.ds(0, 12)],
                    dst_ref=rbuf.at[kz * NX + kx, pl.ds(0, 12)],
                    send_sem=rs_send,
                    recv_sem=rs_recv,
                    device_id=(f, tz * NX + tx),
                    device_id_type=MESH,
                ).start()

        @pl.when(own)
        def _():
            wait_for(rbuf.at[pl.ds(1, 31), pl.ds(0, 12)], rs_recv)
            num, den = snd[mine, x, 0:8], snd[mine, x, 8:12]
            for k in range(1, NZ * NX):
                num = num + rbuf[k, 0:8]
                den = den + rbuf[k, 8:12]
            den = jnp.concatenate([den, den], axis=0)
            now = gbuf[mine, x]
            upd[...] = 0.5 * (now + (num + rho * now) / (den + rho))

            @pl.when(has_up)
            def _():
                pltpu.make_async_remote_copy(
                    src_ref=upd, dst_ref=halo.at[parity, 0],
                    send_sem=ex_send.at[0], recv_sem=ex_recv.at[parity, 0],
                    device_id=(f + 1, bl), device_id_type=MESH,
                ).start()

            @pl.when(has_down)
            def _():
                pltpu.make_async_remote_copy(
                    src_ref=upd, dst_ref=halo.at[parity, 1],
                    send_sem=ex_send.at[1], recv_sem=ex_recv.at[parity, 1],
                    device_id=(f - 1, bl), device_id_type=MESH,
                ).start()

            inner = smooth(upd, 1)

            @pl.when(it > 0)
            def _():
                wait_for(rbuf.at[pl.ds(1, 31), pl.ds(0, 8)], ag_send)

            @pl.when(has_down)
            def _():
                wait_for(halo.at[parity, 0], ex_recv.at[parity, 0])

            @pl.when(has_up)
            def _():
                wait_for(halo.at[parity, 1], ex_recv.at[parity, 1])

            gbuf[mine, x] = inner + smooth(halo.at[parity, 0], 0) + smooth(halo.at[parity, 1], 2)
            for kz, kx in STEPS:
                tz, tx = peer(kz, kx)
                pltpu.make_async_remote_copy(
                    src_ref=gbuf.at[mine, x], dst_ref=gbuf.at[mine, x],
                    send_sem=ag_send, recv_sem=ag_recv,
                    device_id=(f, tz * NX + tx), device_id_type=MESH,
                ).start()
            wait_for(rbuf.at[pl.ds(0, 23), pl.ds(0, 8)], ag_recv)
            wait_for(rbuf.at[pl.ds(0, 23), pl.ds(0, 12)], rs_send)

            @pl.when(has_up)
            def _():
                wait_for(upd, ex_send.at[0])

            @pl.when(has_down)
            def _():
                wait_for(upd, ex_send.at[1])

        @pl.when(not_own)
        def _():
            wait_for(rbuf.at[pl.ds(0, 24), pl.ds(0, 8)], ag_recv)
            wait_for(rbuf.at[pl.ds(0, 24), pl.ds(0, 12)], rs_send)

        return 0

    lax.fori_loop(0, ITERS, sweep, 0)

    @pl.when(own)
    def _():
        wait_for(rbuf.at[pl.ds(1, 31), pl.ds(0, 8)], ag_send)

    out_ref[...] = gbuf[...]


def body(visibilities, predicted_sky, station_pairs, start_gains, kernel_width):
    chans, stations = start_gains.shape[2:]
    blocal = station_pairs.shape[1]
    nf = lax.axis_size("freq")
    rho = float(TIMES * blocal * lax.axis_size("bl") / stations)
    vis = jnp.swapaxes(visibilities, 1, 2).reshape(2, 8, blocal).astype(F32)
    sky = jnp.swapaxes(predicted_sky, 2, 3).reshape(2 * DIRS, 8, blocal).astype(F32)
    whole = pl.BlockSpec(memory_space=pltpu.VMEM)
    gains = pl.pallas_call(
        functools.partial(kernel, nf, rho),
        out_shape=jax.ShapeDtypeStruct((DIRS, BLOCKS, 8, LANE), F32),
        in_specs=[whole, whole, whole, whole, pl.BlockSpec(memory_space=pltpu.SMEM)],
        out_specs=whole,
        scratch_shapes=[
            pltpu.VMEM((DIRS, BLOCKS, 8, LANE), F32),
            pltpu.VMEM((16 * DIRS, STATIONS), BF16),
            pltpu.VMEM((16 * DIRS, 2 * blocal), F32),
            pltpu.VMEM((STATIONS, 2 * blocal), BF16),
            pltpu.VMEM((2 * blocal, STATIONS), BF16),
            pltpu.VMEM((80, 2 * blocal), BF16),
            pltpu.VMEM((DIRS, BLOCKS, 16, LANE), F32),
            pltpu.VMEM((NZ * NX, 16, LANE), F32),
            pltpu.VMEM((2, 2, 8, LANE), F32),
            pltpu.VMEM((8, LANE), F32),
            pltpu.VMEM((3 * CHANS, 8, LANE), F32),
            pltpu.SemaphoreType.DMA,
            pltpu.SemaphoreType.DMA,
            pltpu.SemaphoreType.DMA,
            pltpu.SemaphoreType.DMA,
            pltpu.SemaphoreType.DMA((2,)),
            pltpu.SemaphoreType.DMA((2, 2)),
        ],
        compiler_params=pltpu.CompilerParams(
            collective_id=0, has_side_effects=True, vmem_limit_bytes=48 * 1024 * 1024
        ),
    )(vis, sky, station_pairs, start_gains, kernel_width)
    gains = gains.reshape(DIRS, BLOCKS, 2, chans, LANE)
    return gains.transpose(2, 0, 3, 1, 4).reshape(2, DIRS, chans, stations)


def solution(mesh):
    in_specs = (
        P(None, "freq", None, "bl"),
        P(None, None, "freq", None, "bl"),
        P(None, "bl"),
        P(None, None, "freq", None),
        P(),
    )
    out_specs = P(None, None, "freq", None)
    return jax.shard_map(body, mesh=mesh, in_specs=in_specs, out_specs=out_specs, check_vma=False)
```

```python
import functools

import jax
import jax.numpy as jnp
from jax import lax
from jax.experimental import pallas as pl
from jax.experimental.pallas import tpu as pltpu
from jax.sharding import PartitionSpec as P

ITERS = 4
DIRS = 6
CHANS = 4
TIMES = 2
STATIONS = 512
NZ, NX = 8, 4
LANE = 128
BLOCKS = STATIONS // LANE
MESH = pl.DeviceIdType.MESH
F32, BF16 = jnp.float32, jnp.bfloat16


def hops(kz, kx):
    return min(kz, NZ - kz) + min(kx, NX - kx)


STEPS = sorted(
    [(kz, kx) for kz in range(NZ) for kx in range(NX) if kz or kx], key=lambda k: -hops(*k)
)
X_STEPS = sorted(range(NX), key=lambda kx: -hops(0, kx))


def owner_of(z):
    return jnp.logical_and(z != 3, z != 7), jnp.minimum(jnp.where(z > 3, z - 1, z), DIRS - 1)


def wait_for(ref, sem):
    pltpu.make_async_copy(ref, ref, sem).wait()


def kernel(
    nf, rho, vis_hbm, sky_hbm, ids_hbm, gains_hbm, width_hbm, out_ref,
    vis_raw, sky_raw, ids_ref, gains_ref, width_ref, vis_ref, sky_ref,
    gbuf, gat, oh, terms, snd, rbuf, halo, upd, wts,
    in_sems, rs_send, rs_recv, ag_send, ag_recv, ex_send, ex_recv,
):
    blocal = ids_ref.shape[1]
    f, bl = lax.axis_index("freq"), lax.axis_index("bl")
    z, x = lax.div(bl, NX), lax.rem(bl, NX)
    own, mine = owner_of(z)
    not_own = jnp.logical_not(own)
    has_up, has_down = f < nf - 1, f > 0

    def peer(kz, kx):
        return lax.rem(z + kz, NZ), lax.rem(x + kx, NX)

    halo[...] = jnp.zeros_like(halo)

    barrier = pltpu.get_barrier_semaphore()
    for kz, kx in STEPS:
        tz, tx = peer(kz, kx)
        pl.semaphore_signal(barrier, inc=1, device_id=(f, tz * NX + tx), device_id_type=MESH)
    for step in (1, nf - 1):
        neighbour = lax.rem(f + step, nf)
        pl.semaphore_signal(barrier, inc=1, device_id=(neighbour, bl), device_id_type=MESH)

    loads = [
        pltpu.make_async_copy(src, dst, in_sems.at[i])
        for i, (src, dst) in enumerate(
            [
                (ids_hbm, ids_ref),
                (width_hbm, width_ref),
                (gains_hbm, gains_ref),
                (vis_hbm, vis_raw),
                (sky_hbm, sky_raw),
            ]
        )
    ]
    for load in loads:
        load.start()

    sub = lax.broadcasted_iota(jnp.int32, (8, LANE), 0)
    top = sub < CHANS

    loads[0].wait()

    def fill(i, _):
        for h in range(2):
            row = ids_ref[h : h + 1, pl.ds(pl.multiple_of(i * LANE, LANE), LANE)]
            at = pl.multiple_of(h * blocal + i * LANE, LANE)
            column = jnp.transpose(jnp.broadcast_to(row, (LANE, LANE)))
            for b in range(BLOCKS):
                station = lax.broadcasted_iota(jnp.int32, (LANE, LANE), 1) + b * LANE
                oh[b, pl.ds(at, LANE)] = jnp.where(station == column, 1.0, 0.0).astype(BF16)
        return 0

    lax.fori_loop(0, blocal // LANE, fill, 0)

    loads[1].wait()
    spread = jnp.full((8, LANE), width_ref[mine], jnp.int32).astype(F32)
    chan = jnp.bitwise_and(sub, CHANS - 1)
    taps = []
    for j in range(3 * CHANS):
        shift = j - CHANS - chan
        there = f * CHANS + (j - CHANS)
        inside = (jnp.abs(shift) <= CHANS) & (there >= 0) & (there < nf * CHANS)
        distance = shift.astype(F32)
        taps.append(
            jnp.where(inside, jnp.exp(-(distance * distance) / (2.0 * spread * spread)), 0.0)
        )
    total = functools.reduce(jnp.add, taps)
    for j in range(3 * CHANS):
        wts[j] = taps[j] / total

    loads[2].wait()
    for d in range(DIRS):
        for b in range(BLOCKS):
            lanes = slice(b * LANE, (b + 1) * LANE)
            gbuf[d, b] = jnp.concatenate(
                [gains_ref[0, d, :, lanes], gains_ref[1, d, :, lanes]], axis=0
            )

    loads[3].wait()
    for r in range(2):
        for c in range(CHANS):
            value = vis_raw[r, c].astype(F32)
            for t in range(TIMES):
                vis_ref[r, CHANS * t + c : CHANS * t + c + 1] = value[t : t + 1]
    loads[4].wait()

    def unpack(d, _):
        for r in range(2):
            for c in range(CHANS):
                value = sky_raw[d, r, c].astype(F32)
                for t in range(TIMES):
                    sky_ref[2 * d + r, CHANS * t + c : CHANS * t + c + 1] = value[t : t + 1]
        return 0

    lax.fori_loop(0, DIRS, unpack, 0)

    def swap(tile):
        return pltpu.roll(tile, CHANS, 0)

    def parts_of(tile):
        other = swap(tile)
        return jnp.where(top, tile, other), jnp.where(top, other, tile)

    def fold(a, b):
        return jnp.where(top, a, b) + swap(jnp.where(top, b, a))

    def ends(j):
        found = []
        for h in range(2):
            row = jnp.broadcast_to(ids_ref[h : h + 1, j * LANE : (j + 1) * LANE], (8, LANE))
            found.append((lax.shift_right_logical(row, 7), jnp.bitwise_and(row, LANE - 1)))
        return found

    def taken(d, block, at, lane, other):
        got = jnp.take_along_axis(gbuf[d, block], lane, axis=1)
        return jnp.where(at == block, got, other)

    def gather(steps, start):
        blocks = [lax.rem(x + k, NX) for k in steps]
        for j in range(blocal // LANE):
            for h, (at, lane) in enumerate(ends(j)):
                lanes = slice(h * blocal + j * LANE, h * blocal + (j + 1) * LANE)
                for d in range(DIRS):
                    rows = slice(8 * d, 8 * d + 8)
                    value = jnp.zeros((8, LANE), F32) if start else gat[rows, lanes]
                    for block in blocks:
                        value = taken(d, block, at, lane, value)
                    gat[rows, lanes] = value

    def chunk(j, last):
        lanes = slice(j * LANE, (j + 1) * LANE)
        after = slice(blocal + j * LANE, blocal + (j + 1) * LANE)
        (p_at, p_lane), (q_at, q_lane) = ends(j)
        sum_re, sum_im = vis_ref[0, :, lanes], vis_ref[1, :, lanes]
        kept = []
        for d in range(DIRS):
            rows = slice(8 * d, 8 * d + 8)
            l_re, l_im = parts_of(taken(d, last, p_at, p_lane, gat[rows, lanes]))
            r_re, r_im = parts_of(taken(d, last, q_at, q_lane, gat[rows, after]))
            m_re, m_im = sky_ref[2 * d, :, lanes], sky_ref[2 * d + 1, :, lanes]
            z_re = l_re * m_re - l_im * m_im
            z_im = l_re * m_im + l_im * m_re
            y_re = r_re * m_re + r_im * m_im
            y_im = r_re * m_im - r_im * m_re
            u_re = z_re * r_re + z_im * r_im
            u_im = z_im * r_re - z_re * r_im
            sum_re, sum_im = sum_re - u_re, sum_im - u_im
            kept.append((z_re, z_im, y_re, y_im, u_re, u_im))
        first, second, first_den, second_den = [], [], [], []
        for z_re, z_im, y_re, y_im, u_re, u_im in kept:
            res_re, res_im = sum_re + u_re, sum_im + u_im
            first.append(fold(res_re * y_re + res_im * y_im, res_im * y_re - res_re * y_im))
            second.append(fold(res_re * z_re + res_im * z_im, res_re * z_im - res_im * z_re))
            first_den.append(y_re * y_re + y_im * y_im)
            second_den.append(z_re * z_re + z_im * z_im)
        for d in range(0, DIRS, 2):
            first.append(fold(first_den[d], first_den[d + 1]))
            second.append(fold(second_den[d], second_den[d + 1]))
        pad = jnp.zeros((8, LANE), F32)
        terms[:, lanes] = jnp.concatenate([*first, pad], axis=0).astype(BF16)
        terms[:, after] = jnp.concatenate([*second, pad], axis=0).astype(BF16)

    def row_of(ref, e):
        return jnp.where(
            top,
            jnp.broadcast_to(ref[e : e + 1, :], (8, LANE)),
            jnp.broadcast_to(ref[CHANS + e : CHANS + e + 1, :], (8, LANE)),
        )

    def smooth(ref, side):
        return functools.reduce(
            jnp.add, [wts[side * CHANS + e] * row_of(ref, e) for e in range(CHANS)]
        )

    def finish_sends():
        @pl.when(own)
        def _():
            wait_for(rbuf.at[pl.ds(0, 23), pl.ds(0, 12)], rs_send)
            wait_for(rbuf.at[pl.ds(1, 31), pl.ds(0, 8)], ag_send)

            @pl.when(has_up)
            def _():
                wait_for(upd, ex_send.at[0])

            @pl.when(has_down)
            def _():
                wait_for(upd, ex_send.at[1])

        @pl.when(not_own)
        def _():
            wait_for(rbuf.at[pl.ds(0, 24), pl.ds(0, 12)], rs_send)

    def arrived(step):
        tiles = rbuf.at[pl.ds(0, DIRS), pl.ds(0, 8)]
        if step:
            wait_for(tiles, ag_recv.at[step])
        else:

            @pl.when(own)
            def _():
                wait_for(rbuf.at[pl.ds(0, DIRS - 1), pl.ds(0, 8)], ag_recv.at[0])

            @pl.when(not_own)
            def _():
                wait_for(tiles, ag_recv.at[0])

    def sweep(it, _):
        parity = lax.rem(it, 2)
        groups = ((0,), (1, 3), (2,))
        for group in groups:

            @pl.when(it > 0)
            def _():
                for step in group:
                    arrived(step)

            if group != groups[-1]:
                gather(group, group == groups[0])

        @pl.when(it > 0)
        def _():
            finish_sends()

        last = lax.rem(x + 2, NX)
        for j in range(blocal // LANE):
            chunk(j, last)

        @pl.when(it == 0)
        def _():
            pl.semaphore_wait(barrier, len(STEPS) + 2)

        for kx in X_STEPS:
            tx = lax.rem(x + kx, NX)
            normals = jnp.dot(terms[...], oh[tx], preferred_element_type=F32)
            for d in range(DIRS):
                snd[d, tx, 0:8] = normals[8 * d : 8 * d + 8]
                den = 8 * DIRS + CHANS * d
                snd[d, tx, 8:12] = normals[den : den + CHANS]
            for kz in sorted(range(NZ), key=lambda k: -hops(k, 0)):
                if not (kz or kx):
                    continue
                tz = lax.rem(z + kz, NZ)
                there, which = owner_of(tz)

                @pl.when(there)
                def _():
                    pltpu.make_async_remote_copy(
                        src_ref=snd.at[which, tx, pl.ds(0, 12)],
                        dst_ref=rbuf.at[kz * NX + kx, pl.ds(0, 12)],
                        send_sem=rs_send,
                        recv_sem=rs_recv,
                        device_id=(f, tz * NX + tx),
                        device_id_type=MESH,
                    ).start()

        @pl.when(own)
        def _():
            wait_for(rbuf.at[pl.ds(1, 31), pl.ds(0, 12)], rs_recv)
            num, den = snd[mine, x, 0:8], snd[mine, x, 8:12]
            for k in range(1, NZ * NX):
                num = num + rbuf[k, 0:8]
                den = den + rbuf[k, 8:12]
            den = jnp.concatenate([den, den], axis=0)
            now = gbuf[mine, x]
            upd[...] = 0.5 * (now + (num + rho * now) / (den + rho))

            @pl.when(has_up)
            def _():
                pltpu.make_async_remote_copy(
                    src_ref=upd, dst_ref=halo.at[parity, 0],
                    send_sem=ex_send.at[0], recv_sem=ex_recv.at[parity, 0],
                    device_id=(f + 1, bl), device_id_type=MESH,
                ).start()

            @pl.when(has_down)
            def _():
                pltpu.make_async_remote_copy(
                    src_ref=upd, dst_ref=halo.at[parity, 1],
                    send_sem=ex_send.at[1], recv_sem=ex_recv.at[parity, 1],
                    device_id=(f - 1, bl), device_id_type=MESH,
                ).start()

            inner = smooth(upd, 1)

            @pl.when(has_down)
            def _():
                wait_for(halo.at[parity, 0], ex_recv.at[parity, 0])

            @pl.when(has_up)
            def _():
                wait_for(halo.at[parity, 1], ex_recv.at[parity, 1])

            gbuf[mine, x] = inner + smooth(halo.at[parity, 0], 0) + smooth(halo.at[parity, 1], 2)
            for kz, kx in STEPS:
                tz, tx = peer(kz, kx)
                pltpu.make_async_remote_copy(
                    src_ref=gbuf.at[mine, x], dst_ref=gbuf.at[mine, x],
                    send_sem=ag_send, recv_sem=ag_recv.at[(NX - kx) % NX],
                    device_id=(f, tz * NX + tx), device_id_type=MESH,
                ).start()
        return 0

    lax.fori_loop(0, ITERS, sweep, 0)
    for step in range(NX):
        arrived(step)
    finish_sends()
    out_ref[...] = gbuf[...]


def body(visibilities, predicted_sky, station_pairs, start_gains, kernel_width):
    chans, stations = start_gains.shape[2:]
    blocal = station_pairs.shape[1]
    nf = lax.axis_size("freq")
    rho = float(TIMES * blocal * lax.axis_size("bl") / stations)
    hbm = pl.BlockSpec(memory_space=pltpu.HBM)
    gains = pl.pallas_call(
        functools.partial(kernel, nf, rho),
        out_shape=jax.ShapeDtypeStruct((DIRS, BLOCKS, 8, LANE), F32),
        in_specs=[hbm] * 5,
        out_specs=pl.BlockSpec(memory_space=pltpu.VMEM),
        scratch_shapes=[
            pltpu.VMEM(visibilities.shape, BF16),
            pltpu.VMEM(predicted_sky.shape, BF16),
            pltpu.VMEM(station_pairs.shape, jnp.int32),
            pltpu.VMEM(start_gains.shape, F32),
            pltpu.SMEM(kernel_width.shape, jnp.int32),
            pltpu.VMEM((2, 8, blocal), F32),
            pltpu.VMEM((2 * DIRS, 8, blocal), F32),
            pltpu.VMEM((DIRS, BLOCKS, 8, LANE), F32),
            pltpu.VMEM((8 * DIRS, 2 * blocal), F32),
            pltpu.VMEM((BLOCKS, 2 * blocal, LANE), BF16),
            pltpu.VMEM((80, 2 * blocal), BF16),
            pltpu.VMEM((DIRS, BLOCKS, 16, LANE), F32),
            pltpu.VMEM((NZ * NX, 16, LANE), F32),
            pltpu.VMEM((2, 2, 8, LANE), F32),
            pltpu.VMEM((8, LANE), F32),
            pltpu.VMEM((3 * CHANS, 8, LANE), F32),
            pltpu.SemaphoreType.DMA((5,)),
            pltpu.SemaphoreType.DMA,
            pltpu.SemaphoreType.DMA,
            pltpu.SemaphoreType.DMA,
            pltpu.SemaphoreType.DMA((NX,)),
            pltpu.SemaphoreType.DMA((2,)),
            pltpu.SemaphoreType.DMA((2, 2)),
        ],
        compiler_params=pltpu.CompilerParams(
            collective_id=0, has_side_effects=True, vmem_limit_bytes=63 * 1024 * 1024
        ),
    )(visibilities, predicted_sky, station_pairs, start_gains, kernel_width)
    gains = gains.reshape(DIRS, BLOCKS, 2, chans, LANE)
    return gains.transpose(2, 0, 3, 1, 4).reshape(2, DIRS, chans, stations)


def solution(mesh):
    in_specs = (
        P(None, "freq", None, "bl"),
        P(None, None, "freq", None, "bl"),
        P(None, "bl"),
        P(None, None, "freq", None),
        P(),
    )
    out_specs = P(None, None, "freq", None)
    return jax.shard_map(body, mesh=mesh, in_specs=in_specs, out_specs=out_specs, check_vma=False)
```

```python
import functools

import jax
import jax.numpy as jnp
from jax import lax
from jax.experimental import pallas as pl
from jax.experimental.pallas import tpu as pltpu
from jax.sharding import PartitionSpec as P

ITERS = 4
DIRS = 6
CHANS = 4
TIMES = 2
STATIONS = 512
NZ, NX = 8, 4
LANE = 128
BLOCKS = STATIONS // LANE
MESH = pl.DeviceIdType.MESH
F32, BF16 = jnp.float32, jnp.bfloat16


def hops(kz, kx):
    return min(kz, NZ - kz) + min(kx, NX - kx)


STEPS = sorted(
    [(kz, kx) for kz in range(NZ) for kx in range(NX) if kz or kx], key=lambda k: -hops(*k)
)
X_STEPS = sorted(range(NX), key=lambda kx: -hops(0, kx))


def owner_of(z):
    return jnp.logical_and(z != 3, z != 7), jnp.minimum(jnp.where(z > 3, z - 1, z), DIRS - 1)


def wait_for(ref, sem):
    pltpu.make_async_copy(ref, ref, sem).wait()


def kernel(
    nf, rho, vis_hbm, sky_hbm, ids_hbm, gains_hbm, width_hbm, out_ref,
    vis_raw, sky_raw, ids_ref, gains_ref, width_ref, vis_ref, sky_ref,
    gbuf, gat, oh, terms, snd, rbuf, halo, upd, wts,
    in_sems, rs_send, rs_recv, ag_send, ag_recv, ex_send, ex_recv,
):
    blocal = ids_ref.shape[1]
    f, bl = lax.axis_index("freq"), lax.axis_index("bl")
    z, x = lax.div(bl, NX), lax.rem(bl, NX)
    own, mine = owner_of(z)
    not_own = jnp.logical_not(own)
    has_up, has_down = f < nf - 1, f > 0

    def peer(kz, kx):
        return lax.rem(z + kz, NZ), lax.rem(x + kx, NX)

    halo[...] = jnp.zeros_like(halo)

    barrier = pltpu.get_barrier_semaphore()
    for kz, kx in STEPS:
        tz, tx = peer(kz, kx)
        pl.semaphore_signal(barrier, inc=1, device_id=(f, tz * NX + tx), device_id_type=MESH)
    for step in (1, nf - 1):
        neighbour = lax.rem(f + step, nf)
        pl.semaphore_signal(barrier, inc=1, device_id=(neighbour, bl), device_id_type=MESH)

    loads = [
        pltpu.make_async_copy(src, dst, in_sems.at[i])
        for i, (src, dst) in enumerate(
            [
                (ids_hbm, ids_ref),
                (width_hbm, width_ref),
                (gains_hbm, gains_ref),
                (vis_hbm, vis_raw),
                (sky_hbm, sky_raw),
            ]
        )
    ]
    for load in loads:
        load.start()

    sub = lax.broadcasted_iota(jnp.int32, (8, LANE), 0)
    top = sub < CHANS

    loads[0].wait()

    def fill(i, _):
        for h in range(2):
            row = ids_ref[h : h + 1, pl.ds(pl.multiple_of(i * LANE, LANE), LANE)]
            at = pl.multiple_of(h * blocal + i * LANE, LANE)
            column = jnp.transpose(jnp.broadcast_to(row, (LANE, LANE)))
            for b in range(BLOCKS):
                station = lax.broadcasted_iota(jnp.int32, (LANE, LANE), 1) + b * LANE
                oh[b, pl.ds(at, LANE)] = jnp.where(station == column, 1.0, 0.0).astype(BF16)
        return 0

    lax.fori_loop(0, blocal // LANE, fill, 0)

    loads[1].wait()
    spread = jnp.full((8, LANE), width_ref[mine], jnp.int32).astype(F32)
    chan = jnp.bitwise_and(sub, CHANS - 1)
    taps = []
    for j in range(3 * CHANS):
        shift = j - CHANS - chan
        there = f * CHANS + (j - CHANS)
        inside = (jnp.abs(shift) <= CHANS) & (there >= 0) & (there < nf * CHANS)
        distance = shift.astype(F32)
        taps.append(
            jnp.where(inside, jnp.exp(-(distance * distance) / (2.0 * spread * spread)), 0.0)
        )
    total = functools.reduce(jnp.add, taps)
    for j in range(3 * CHANS):
        wts[j] = taps[j] / total

    loads[2].wait()
    for d in range(DIRS):
        for b in range(BLOCKS):
            lanes = slice(b * LANE, (b + 1) * LANE)
            gbuf[d, b] = jnp.concatenate(
                [gains_ref[0, d, :, lanes], gains_ref[1, d, :, lanes]], axis=0
            )

    loads[3].wait()
    for r in range(2):
        for c in range(CHANS):
            value = vis_raw[r, c].astype(F32)
            for t in range(TIMES):
                vis_ref[r, CHANS * t + c : CHANS * t + c + 1] = value[t : t + 1]
    loads[4].wait()

    def unpack(d, _):
        for r in range(2):
            for c in range(CHANS):
                value = sky_raw[d, r, c].astype(F32)
                for t in range(TIMES):
                    sky_ref[2 * d + r, CHANS * t + c : CHANS * t + c + 1] = value[t : t + 1]
        return 0

    lax.fori_loop(0, DIRS, unpack, 0)

    def swap(tile):
        return pltpu.roll(tile, CHANS, 0)

    def parts_of(tile):
        other = swap(tile)
        return jnp.where(top, tile, other), jnp.where(top, other, tile)

    def fold(a, b):
        return jnp.where(top, a, b) + swap(jnp.where(top, b, a))

    def ends(j):
        found = []
        for h in range(2):
            row = jnp.broadcast_to(ids_ref[h : h + 1, j * LANE : (j + 1) * LANE], (8, LANE))
            found.append((lax.shift_right_logical(row, 7), jnp.bitwise_and(row, LANE - 1)))
        return found

    def taken(d, block, at, lane, other):
        got = jnp.take_along_axis(gbuf[d, block], lane, axis=1)
        return jnp.where(at == block, got, other)

    def gather(steps, start):
        blocks = [lax.rem(x + k, NX) for k in steps]
        for j in range(blocal // LANE):
            for h, (at, lane) in enumerate(ends(j)):
                lanes = slice(h * blocal + j * LANE, h * blocal + (j + 1) * LANE)
                for d in range(DIRS):
                    rows = slice(8 * d, 8 * d + 8)
                    value = jnp.zeros((8, LANE), F32) if start else gat[rows, lanes]
                    for block in blocks:
                        value = taken(d, block, at, lane, value)
                    gat[rows, lanes] = value

    def chunk(j, last):
        lanes = slice(j * LANE, (j + 1) * LANE)
        after = slice(blocal + j * LANE, blocal + (j + 1) * LANE)
        (p_at, p_lane), (q_at, q_lane) = ends(j)
        sum_re, sum_im = vis_ref[0, :, lanes], vis_ref[1, :, lanes]
        kept = []
        for d in range(DIRS):
            rows = slice(8 * d, 8 * d + 8)
            l_re, l_im = parts_of(taken(d, last, p_at, p_lane, gat[rows, lanes]))
            r_re, r_im = parts_of(taken(d, last, q_at, q_lane, gat[rows, after]))
            m_re, m_im = sky_ref[2 * d, :, lanes], sky_ref[2 * d + 1, :, lanes]
            z_re = l_re * m_re - l_im * m_im
            z_im = l_re * m_im + l_im * m_re
            y_re = r_re * m_re + r_im * m_im
            y_im = r_re * m_im - r_im * m_re
            u_re = z_re * r_re + z_im * r_im
            u_im = z_im * r_re - z_re * r_im
            sum_re, sum_im = sum_re - u_re, sum_im - u_im
            kept.append((z_re, z_im, y_re, y_im, u_re, u_im))
        first, second, first_den, second_den = [], [], [], []
        for z_re, z_im, y_re, y_im, u_re, u_im in kept:
            res_re, res_im = sum_re + u_re, sum_im + u_im
            first.append(fold(res_re * y_re + res_im * y_im, res_im * y_re - res_re * y_im))
            second.append(fold(res_re * z_re + res_im * z_im, res_re * z_im - res_im * z_re))
            first_den.append(y_re * y_re + y_im * y_im)
            second_den.append(z_re * z_re + z_im * z_im)
        for d in range(0, DIRS, 2):
            first.append(fold(first_den[d], first_den[d + 1]))
            second.append(fold(second_den[d], second_den[d + 1]))
        pad = jnp.zeros((8, LANE), F32)
        terms[:, lanes] = jnp.concatenate([*first, pad], axis=0).astype(BF16)
        terms[:, after] = jnp.concatenate([*second, pad], axis=0).astype(BF16)

    def row_of(ref, e):
        return jnp.where(
            top,
            jnp.broadcast_to(ref[e : e + 1, :], (8, LANE)),
            jnp.broadcast_to(ref[CHANS + e : CHANS + e + 1, :], (8, LANE)),
        )

    def smooth(ref, side):
        return functools.reduce(
            jnp.add, [wts[side * CHANS + e] * row_of(ref, e) for e in range(CHANS)]
        )

    def finish_sends():
        @pl.when(own)
        def _():
            wait_for(rbuf.at[pl.ds(0, 23), pl.ds(0, 12)], rs_send)
            wait_for(rbuf.at[pl.ds(1, 31), pl.ds(0, 8)], ag_send)

            @pl.when(has_up)
            def _():
                wait_for(upd, ex_send.at[0])

            @pl.when(has_down)
            def _():
                wait_for(upd, ex_send.at[1])

        @pl.when(not_own)
        def _():
            wait_for(rbuf.at[pl.ds(0, 24), pl.ds(0, 12)], rs_send)

    def arrived(step):
        tiles = rbuf.at[pl.ds(0, DIRS), pl.ds(0, 8)]
        if step:
            wait_for(tiles, ag_recv.at[step])
        else:

            @pl.when(own)
            def _():
                wait_for(rbuf.at[pl.ds(0, DIRS - 1), pl.ds(0, 8)], ag_recv.at[0])

            @pl.when(not_own)
            def _():
                wait_for(tiles, ag_recv.at[0])

    def sweep(it, _):
        parity = lax.rem(it, 2)
        groups = ((0,), (1, 3), (2,))
        for group in groups:

            @pl.when(it > 0)
            def _():
                for step in group:
                    arrived(step)

            if group != groups[-1]:
                gather(group, group == groups[0])

        @pl.when(it > 0)
        def _():
            finish_sends()

        last = lax.rem(x + 2, NX)
        for j in range(blocal // LANE):
            chunk(j, last)

        @pl.when(it == 0)
        def _():
            pl.semaphore_wait(barrier, len(STEPS) + 2)

        for kx in X_STEPS:
            tx = lax.rem(x + kx, NX)
            normals = jnp.dot(terms[...], oh[tx], preferred_element_type=F32)
            for d in range(DIRS):
                snd[d, tx, 0:8] = normals[8 * d : 8 * d + 8]
                den = 8 * DIRS + CHANS * d
                snd[d, tx, 8:12] = normals[den : den + CHANS]
            for kz in sorted(range(NZ), key=lambda k: -hops(k, 0)):
                if not (kz or kx):
                    continue
                tz = lax.rem(z + kz, NZ)
                there, which = owner_of(tz)

                @pl.when(there)
                def _():
                    pltpu.make_async_remote_copy(
                        src_ref=snd.at[which, tx, pl.ds(0, 12)],
                        dst_ref=rbuf.at[kz * NX + kx, pl.ds(0, 12)],
                        send_sem=rs_send,
                        recv_sem=rs_recv,
                        device_id=(f, tz * NX + tx),
                        device_id_type=MESH,
                    ).start()

        @pl.when(own)
        def _():
            wait_for(rbuf.at[pl.ds(1, 31), pl.ds(0, 12)], rs_recv)
            num, den = snd[mine, x, 0:8], snd[mine, x, 8:12]
            for k in range(1, NZ * NX):
                num = num + rbuf[k, 0:8]
                den = den + rbuf[k, 8:12]
            den = jnp.concatenate([den, den], axis=0)
            now = gbuf[mine, x]
            upd[...] = 0.5 * (now + (num + rho * now) / (den + rho))

            @pl.when(has_up)
            def _():
                pltpu.make_async_remote_copy(
                    src_ref=upd, dst_ref=halo.at[parity, 0],
                    send_sem=ex_send.at[0], recv_sem=ex_recv.at[parity, 0],
                    device_id=(f + 1, bl), device_id_type=MESH,
                ).start()

            @pl.when(has_down)
            def _():
                pltpu.make_async_remote_copy(
                    src_ref=upd, dst_ref=halo.at[parity, 1],
                    send_sem=ex_send.at[1], recv_sem=ex_recv.at[parity, 1],
                    device_id=(f - 1, bl), device_id_type=MESH,
                ).start()

            inner = smooth(upd, 1)

            @pl.when(has_down)
            def _():
                wait_for(halo.at[parity, 0], ex_recv.at[parity, 0])

            @pl.when(has_up)
            def _():
                wait_for(halo.at[parity, 1], ex_recv.at[parity, 1])

            gbuf[mine, x] = inner + smooth(halo.at[parity, 0], 0) + smooth(halo.at[parity, 1], 2)
            for kz, kx in STEPS:
                tz, tx = peer(kz, kx)
                pltpu.make_async_remote_copy(
                    src_ref=gbuf.at[mine, x], dst_ref=gbuf.at[mine, x],
                    send_sem=ag_send, recv_sem=ag_recv.at[(NX - kx) % NX],
                    device_id=(f, tz * NX + tx), device_id_type=MESH,
                ).start()
        return 0

    lax.fori_loop(0, ITERS, sweep, 0)
    for step in range(NX):
        arrived(step)
    finish_sends()
    for d in range(DIRS):
        for b in range(BLOCKS):
            for part in range(2):
                rows = slice(CHANS * part, CHANS * part + CHANS)
                out_ref[part, d, :, b * LANE : (b + 1) * LANE] = gbuf[d, b, rows]


def body(visibilities, predicted_sky, station_pairs, start_gains, kernel_width):
    chans, stations = start_gains.shape[2:]
    blocal = station_pairs.shape[1]
    nf = lax.axis_size("freq")
    rho = float(TIMES * blocal * lax.axis_size("bl") / stations)
    hbm = pl.BlockSpec(memory_space=pltpu.HBM)
    gains = pl.pallas_call(
        functools.partial(kernel, nf, rho),
        out_shape=jax.ShapeDtypeStruct(start_gains.shape, F32),
        in_specs=[hbm] * 5,
        out_specs=pl.BlockSpec(memory_space=pltpu.VMEM),
        scratch_shapes=[
            pltpu.VMEM(visibilities.shape, BF16),
            pltpu.VMEM(predicted_sky.shape, BF16),
            pltpu.VMEM(station_pairs.shape, jnp.int32),
            pltpu.VMEM(start_gains.shape, F32),
            pltpu.SMEM(kernel_width.shape, jnp.int32),
            pltpu.VMEM((2, 8, blocal), F32),
            pltpu.VMEM((2 * DIRS, 8, blocal), F32),
            pltpu.VMEM((DIRS, BLOCKS, 8, LANE), F32),
            pltpu.VMEM((8 * DIRS, 2 * blocal), F32),
            pltpu.VMEM((BLOCKS, 2 * blocal, LANE), BF16),
            pltpu.VMEM((80, 2 * blocal), BF16),
            pltpu.VMEM((DIRS, BLOCKS, 16, LANE), F32),
            pltpu.VMEM((NZ * NX, 16, LANE), F32),
            pltpu.VMEM((2, 2, 8, LANE), F32),
            pltpu.VMEM((8, LANE), F32),
            pltpu.VMEM((3 * CHANS, 8, LANE), F32),
            pltpu.SemaphoreType.DMA((5,)),
            pltpu.SemaphoreType.DMA,
            pltpu.SemaphoreType.DMA,
            pltpu.SemaphoreType.DMA,
            pltpu.SemaphoreType.DMA((NX,)),
            pltpu.SemaphoreType.DMA((2,)),
            pltpu.SemaphoreType.DMA((2, 2)),
        ],
        compiler_params=pltpu.CompilerParams(
            collective_id=0, has_side_effects=True, vmem_limit_bytes=40 * 1024 * 1024
        ),
    )(*[pltpu.with_memory_space_constraint(v, pltpu.HBM) for v in (visibilities, predicted_sky, station_pairs, start_gains, kernel_width)])
    return gains


def solution(mesh):
    in_specs = (
        P(None, "freq", None, "bl"),
        P(None, None, "freq", None, "bl"),
        P(None, "bl"),
        P(None, None, "freq", None),
        P(),
    )
    out_specs = P(None, None, "freq", None)
    return jax.shard_map(body, mesh=mesh, in_specs=in_specs, out_specs=out_specs, check_vma=False)
```

```python
import functools

import jax
import jax.numpy as jnp
from jax import lax
from jax.experimental import pallas as pl
from jax.experimental.pallas import tpu as pltpu
from jax.sharding import PartitionSpec as P

ITERS = 4
DIRS = 6
CHANS = 4
TIMES = 2
STATIONS = 512
NZ, NX = 8, 4
LANE = 128
BLOCKS = STATIONS // LANE
MESH = pl.DeviceIdType.MESH
F32, BF16 = jnp.float32, jnp.bfloat16


def hops(kz, kx):
    return min(kz, NZ - kz) + min(kx, NX - kx)


STEPS = sorted(
    [(kz, kx) for kz in range(NZ) for kx in range(NX) if kz or kx], key=lambda k: -hops(*k)
)
GROUPS = ((2,), (1, 3), (0,))
ARRIVALS = ((0,), (1,), (3, 2))


def owner_of(z, x):
    idle = lax.rem(x + 3, NX)
    rank = z - jnp.where(z > idle, 1, 0) - jnp.where(z > idle + NX, 1, 0)
    return lax.rem(z, NX) != idle, jnp.minimum(rank, DIRS - 1)


def wait_for(ref, sem):
    pltpu.make_async_copy(ref, ref, sem).wait()


def kernel(
    nf, rho, vis_hbm, sky_hbm, ids_hbm, gains_hbm, width_hbm, out_ref,
    vis_raw, sky_raw, ids_ref, gains_ref, width_ref, vis_ref, sky_ref,
    gbuf, gat, oh, terms, snd, rbuf, halo, upd, wts,
    in_sems, rs_send, rs_recv, ag_send, ag_recv, ex_send, ex_recv,
):
    blocal = ids_ref.shape[1]
    f, bl = lax.axis_index("freq"), lax.axis_index("bl")
    z, x = lax.div(bl, NX), lax.rem(bl, NX)
    own, mine = owner_of(z, x)
    not_own = jnp.logical_not(own)
    has_up, has_down = f < nf - 1, f > 0

    def peer(kz, kx):
        return lax.rem(z + kz, NZ), lax.rem(x + kx, NX)

    halo[...] = jnp.zeros_like(halo)

    barrier = pltpu.get_barrier_semaphore()
    for kz, kx in STEPS:
        tz, tx = peer(kz, kx)
        pl.semaphore_signal(barrier, inc=1, device_id=(f, tz * NX + tx), device_id_type=MESH)
    for step in (1, nf - 1):
        neighbour = lax.rem(f + step, nf)
        pl.semaphore_signal(barrier, inc=1, device_id=(neighbour, bl), device_id_type=MESH)

    loads = [
        pltpu.make_async_copy(src, dst, in_sems.at[i])
        for i, (src, dst) in enumerate(
            [
                (ids_hbm, ids_ref),
                (width_hbm, width_ref),
                (gains_hbm, gains_ref),
                (vis_hbm, vis_raw),
                (sky_hbm, sky_raw),
            ]
        )
    ]
    for load in loads:
        load.start()

    sub = lax.broadcasted_iota(jnp.int32, (8, LANE), 0)
    top = sub < CHANS

    loads[0].wait()

    def fill(i, _):
        for h in range(2):
            row = ids_ref[h : h + 1, pl.ds(pl.multiple_of(i * LANE, LANE), LANE)]
            at = pl.multiple_of(h * blocal + i * LANE, LANE)
            column = jnp.transpose(jnp.broadcast_to(row, (LANE, LANE)))
            for b in range(BLOCKS):
                station = lax.broadcasted_iota(jnp.int32, (LANE, LANE), 1) + b * LANE
                oh[b, pl.ds(at, LANE)] = jnp.where(station == column, 1.0, 0.0).astype(BF16)
        return 0

    lax.fori_loop(0, blocal // LANE, fill, 0)

    loads[1].wait()
    spread = jnp.full((8, LANE), width_ref[mine], jnp.int32).astype(F32)
    chan = jnp.bitwise_and(sub, CHANS - 1)
    taps = []
    for j in range(3 * CHANS):
        shift = j - CHANS - chan
        there = f * CHANS + (j - CHANS)
        inside = (jnp.abs(shift) <= CHANS) & (there >= 0) & (there < nf * CHANS)
        distance = shift.astype(F32)
        taps.append(
            jnp.where(inside, jnp.exp(-(distance * distance) / (2.0 * spread * spread)), 0.0)
        )
    total = functools.reduce(jnp.add, taps)
    for j in range(3 * CHANS):
        wts[j] = taps[j] / total

    loads[2].wait()
    for d in range(DIRS):
        for b in range(BLOCKS):
            lanes = slice(b * LANE, (b + 1) * LANE)
            gbuf[d, b] = jnp.concatenate(
                [gains_ref[0, d, :, lanes], gains_ref[1, d, :, lanes]], axis=0
            )

    loads[3].wait()
    for r in range(2):
        for c in range(CHANS):
            value = vis_raw[r, c].astype(F32)
            for t in range(TIMES):
                vis_ref[r, CHANS * t + c : CHANS * t + c + 1] = value[t : t + 1]
    loads[4].wait()

    def unpack(d, _):
        for r in range(2):
            for c in range(CHANS):
                value = sky_raw[d, r, c].astype(F32)
                for t in range(TIMES):
                    sky_ref[2 * d + r, CHANS * t + c : CHANS * t + c + 1] = value[t : t + 1]
        return 0

    lax.fori_loop(0, DIRS, unpack, 0)

    def swap(tile):
        return pltpu.roll(tile, CHANS, 0)

    def parts_of(tile):
        other = swap(tile)
        return jnp.where(top, tile, other), jnp.where(top, other, tile)

    def fold(a, b):
        return jnp.where(top, a, b) + swap(jnp.where(top, b, a))

    def ends(j):
        found = []
        for h in range(2):
            row = jnp.broadcast_to(ids_ref[h : h + 1, j * LANE : (j + 1) * LANE], (8, LANE))
            found.append((lax.shift_right_logical(row, 7), jnp.bitwise_and(row, LANE - 1)))
        return found

    def taken(d, blocks, at, lane, value):
        for block in blocks:
            got = jnp.take_along_axis(gbuf[d, block], lane, axis=1)
            value = got if value is None else jnp.where(at == block, got, value)
        return value

    def gather(steps, start):
        blocks = [lax.rem(x + k, NX) for k in steps]
        for j in range(blocal // LANE):
            for h, (at, lane) in enumerate(ends(j)):
                lanes = slice(h * blocal + j * LANE, h * blocal + (j + 1) * LANE)
                for d in range(DIRS):
                    rows = slice(8 * d, 8 * d + 8)
                    gat[rows, lanes] = taken(
                        d, blocks, at, lane, None if start else gat[rows, lanes]
                    )

    def chunk(j, last):
        lanes = slice(j * LANE, (j + 1) * LANE)
        after = slice(blocal + j * LANE, blocal + (j + 1) * LANE)
        (p_at, p_lane), (q_at, q_lane) = ends(j)
        sum_re, sum_im = vis_ref[0, :, lanes], vis_ref[1, :, lanes]
        kept = []
        for d in range(DIRS):
            rows = slice(8 * d, 8 * d + 8)
            l_re, l_im = parts_of(taken(d, last, p_at, p_lane, gat[rows, lanes]))
            r_re, r_im = parts_of(taken(d, last, q_at, q_lane, gat[rows, after]))
            m_re, m_im = sky_ref[2 * d, :, lanes], sky_ref[2 * d + 1, :, lanes]
            z_re = l_re * m_re - l_im * m_im
            z_im = l_re * m_im + l_im * m_re
            y_re = r_re * m_re + r_im * m_im
            y_im = r_re * m_im - r_im * m_re
            u_re = z_re * r_re + z_im * r_im
            u_im = z_im * r_re - z_re * r_im
            sum_re, sum_im = sum_re - u_re, sum_im - u_im
            kept.append((z_re, z_im, y_re, y_im, u_re, u_im))
        first, second, first_den, second_den = [], [], [], []
        for z_re, z_im, y_re, y_im, u_re, u_im in kept:
            res_re, res_im = sum_re + u_re, sum_im + u_im
            first.append(fold(res_re * y_re + res_im * y_im, res_im * y_re - res_re * y_im))
            second.append(fold(res_re * z_re + res_im * z_im, res_re * z_im - res_im * z_re))
            first_den.append(y_re * y_re + y_im * y_im)
            second_den.append(z_re * z_re + z_im * z_im)
        for d in range(0, DIRS, 2):
            first.append(fold(first_den[d], first_den[d + 1]))
            second.append(fold(second_den[d], second_den[d + 1]))
        pad = jnp.zeros((8, LANE), F32)
        terms[:, lanes] = jnp.concatenate([*first, pad], axis=0).astype(BF16)
        terms[:, after] = jnp.concatenate([*second, pad], axis=0).astype(BF16)

    def row_of(ref, e):
        return jnp.where(
            top,
            jnp.broadcast_to(ref[e : e + 1, :], (8, LANE)),
            jnp.broadcast_to(ref[CHANS + e : CHANS + e + 1, :], (8, LANE)),
        )

    def smooth(ref, side):
        return functools.reduce(
            jnp.add, [wts[side * CHANS + e] * row_of(ref, e) for e in range(CHANS)]
        )

    def finish_sends():
        @pl.when(own)
        def _():
            wait_for(rbuf.at[pl.ds(0, 23), pl.ds(0, 12)], rs_send)
            wait_for(rbuf.at[pl.ds(1, 31), pl.ds(0, 8)], ag_send)

            @pl.when(has_up)
            def _():
                wait_for(upd, ex_send.at[0])

            @pl.when(has_down)
            def _():
                wait_for(upd, ex_send.at[1])

        @pl.when(not_own)
        def _():
            wait_for(rbuf.at[pl.ds(0, 24), pl.ds(0, 12)], rs_send)

    def arrived(step):
        tiles = rbuf.at[pl.ds(0, DIRS), pl.ds(0, 8)]
        if step:
            wait_for(tiles, ag_recv.at[step])
        else:

            @pl.when(own)
            def _():
                wait_for(rbuf.at[pl.ds(0, DIRS - 1), pl.ds(0, 8)], ag_recv.at[0])

            @pl.when(not_own)
            def _():
                wait_for(tiles, ag_recv.at[0])

    def sweep(it, _):
        parity = lax.rem(it, 2)
        for group in ARRIVALS:

            @pl.when(it > 0)
            def _():
                for step in group:
                    arrived(step)

            if group != ARRIVALS[-1]:
                gather(group, group == ARRIVALS[0])

        @pl.when(it > 0)
        def _():
            finish_sends()

        last = [lax.rem(x + k, NX) for k in ARRIVALS[-1]]
        for j in range(blocal // LANE):
            chunk(j, last)

        for group in GROUPS:
            for kx in group:
                tx = lax.rem(x + kx, NX)
                normals = jnp.dot(terms[...], oh[tx], preferred_element_type=F32)
                for d in range(DIRS):
                    snd[d, tx, 0:8] = normals[8 * d : 8 * d + 8]
                    den = 8 * DIRS + CHANS * d
                    snd[d, tx, 8:12] = normals[den : den + CHANS]
            if group == GROUPS[0]:

                @pl.when(it == 0)
                def _():
                    pl.semaphore_wait(barrier, len(STEPS) + 2)

            for kz, kx in sorted(
                [(kz, kx) for kz in range(NZ) for kx in group if kz or kx],
                key=lambda k: -hops(*k),
            ):
                tz, tx = peer(kz, kx)
                there, which = owner_of(tz, tx)

                @pl.when(there)
                def _():
                    pltpu.make_async_remote_copy(
                        src_ref=snd.at[which, tx, pl.ds(0, 12)],
                        dst_ref=rbuf.at[kz * NX + kx, pl.ds(0, 12)],
                        send_sem=rs_send,
                        recv_sem=rs_recv,
                        device_id=(f, tz * NX + tx),
                        device_id_type=MESH,
                    ).start()

        @pl.when(own)
        def _():
            wait_for(rbuf.at[pl.ds(1, 31), pl.ds(0, 12)], rs_recv)
            num, den = snd[mine, x, 0:8], snd[mine, x, 8:12]
            for k in range(1, NZ * NX):
                num = num + rbuf[k, 0:8]
                den = den + rbuf[k, 8:12]
            den = jnp.concatenate([den, den], axis=0)
            now = gbuf[mine, x]
            upd[...] = 0.5 * (now + (num + rho * now) / (den + rho))

            @pl.when(has_up)
            def _():
                pltpu.make_async_remote_copy(
                    src_ref=upd, dst_ref=halo.at[parity, 0],
                    send_sem=ex_send.at[0], recv_sem=ex_recv.at[parity, 0],
                    device_id=(f + 1, bl), device_id_type=MESH,
                ).start()

            @pl.when(has_down)
            def _():
                pltpu.make_async_remote_copy(
                    src_ref=upd, dst_ref=halo.at[parity, 1],
                    send_sem=ex_send.at[1], recv_sem=ex_recv.at[parity, 1],
                    device_id=(f - 1, bl), device_id_type=MESH,
                ).start()

            inner = smooth(upd, 1)

            @pl.when(has_down)
            def _():
                wait_for(halo.at[parity, 0], ex_recv.at[parity, 0])

            @pl.when(has_up)
            def _():
                wait_for(halo.at[parity, 1], ex_recv.at[parity, 1])

            gbuf[mine, x] = inner + smooth(halo.at[parity, 0], 0) + smooth(halo.at[parity, 1], 2)
            for kz, kx in sorted(STEPS, key=lambda k: (-hops(k[0], 0), -hops(0, k[1]))):
                tz, tx = peer(kz, kx)
                pltpu.make_async_remote_copy(
                    src_ref=gbuf.at[mine, x], dst_ref=gbuf.at[mine, x],
                    send_sem=ag_send, recv_sem=ag_recv.at[(NX - kx) % NX],
                    device_id=(f, tz * NX + tx), device_id_type=MESH,
                ).start()
        return 0

    lax.fori_loop(0, ITERS, sweep, 0)
    for step in range(NX):
        arrived(step)
    finish_sends()
    for d in range(DIRS):
        for b in range(BLOCKS):
            for part in range(2):
                rows = slice(CHANS * part, CHANS * part + CHANS)
                out_ref[part, d, :, b * LANE : (b + 1) * LANE] = gbuf[d, b, rows]


def body(visibilities, predicted_sky, station_pairs, start_gains, kernel_width):
    chans, stations = start_gains.shape[2:]
    blocal = station_pairs.shape[1]
    nf = lax.axis_size("freq")
    rho = float(TIMES * blocal * lax.axis_size("bl") / stations)
    hbm = pl.BlockSpec(memory_space=pltpu.HBM)
    gains = pl.pallas_call(
        functools.partial(kernel, nf, rho),
        out_shape=jax.ShapeDtypeStruct(start_gains.shape, F32),
        in_specs=[hbm] * 5,
        out_specs=pl.BlockSpec(memory_space=pltpu.VMEM),
        scratch_shapes=[
            pltpu.VMEM(visibilities.shape, BF16),
            pltpu.VMEM(predicted_sky.shape, BF16),
            pltpu.VMEM(station_pairs.shape, jnp.int32),
            pltpu.VMEM(start_gains.shape, F32),
            pltpu.SMEM(kernel_width.shape, jnp.int32),
            pltpu.VMEM((2, 8, blocal), F32),
            pltpu.VMEM((2 * DIRS, 8, blocal), F32),
            pltpu.VMEM((DIRS, BLOCKS, 8, LANE), F32),
            pltpu.VMEM((8 * DIRS, 2 * blocal), F32),
            pltpu.VMEM((BLOCKS, 2 * blocal, LANE), BF16),
            pltpu.VMEM((80, 2 * blocal), BF16),
            pltpu.VMEM((DIRS, BLOCKS, 16, LANE), F32),
            pltpu.VMEM((NZ * NX, 16, LANE), F32),
            pltpu.VMEM((2, 2, 8, LANE), F32),
            pltpu.VMEM((8, LANE), F32),
            pltpu.VMEM((3 * CHANS, 8, LANE), F32),
            pltpu.SemaphoreType.DMA((5,)),
            pltpu.SemaphoreType.DMA,
            pltpu.SemaphoreType.DMA,
            pltpu.SemaphoreType.DMA,
            pltpu.SemaphoreType.DMA((NX,)),
            pltpu.SemaphoreType.DMA((2,)),
            pltpu.SemaphoreType.DMA((2, 2)),
        ],
        compiler_params=pltpu.CompilerParams(
            collective_id=0, has_side_effects=True, vmem_limit_bytes=40 * 1024 * 1024
        ),
    )(*[pltpu.with_memory_space_constraint(v, pltpu.HBM) for v in (visibilities, predicted_sky, station_pairs, start_gains, kernel_width)])
    return gains


def solution(mesh):
    in_specs = (
        P(None, "freq", None, "bl"),
        P(None, None, "freq", None, "bl"),
        P(None, "bl"),
        P(None, None, "freq", None),
        P(),
    )
    out_specs = P(None, None, "freq", None)
    return jax.shard_map(body, mesh=mesh, in_specs=in_specs, out_specs=out_specs, check_vma=False)
```

```python
import functools

import jax
import jax.numpy as jnp
from jax import lax
from jax.experimental import pallas as pl
from jax.experimental.pallas import tpu as pltpu
from jax.sharding import PartitionSpec as P

ITERS = 4
DIRS = 6
CHANS = 4
TIMES = 2
STATIONS = 512
NZ, NX = 8, 4
LANE = 128
BLOCKS = STATIONS // LANE
MESH = pl.DeviceIdType.MESH
F32, BF16 = jnp.float32, jnp.bfloat16


def hops(kz, kx):
    return min(kz, NZ - kz) + min(kx, NX - kx)


STEPS = sorted(
    [(kz, kx) for kz in range(NZ) for kx in range(NX) if kz or kx], key=lambda k: -hops(*k)
)
GROUPS = ((2,), (1, 3), (0,))
SUMS = (1, 3, 0, 2)
ARRIVALS = ((0,), (1,), (3, 2))


def owner_of(z, x):
    idle = lax.rem(x + 3, NX)
    rank = z - jnp.where(z > idle, 1, 0) - jnp.where(z > idle + NX, 1, 0)
    return lax.rem(z, NX) != idle, jnp.minimum(rank, DIRS - 1)


def tree(values):
    while len(values) > 1:
        values = [
            values[i] + values[i + 1] if i + 1 < len(values) else values[i]
            for i in range(0, len(values), 2)
        ]
    return values[0]


def wait_for(ref, sem):
    pltpu.make_async_copy(ref, ref, sem).wait()


def kernel(
    nf, rho, vis_hbm, sky_hbm, ids_hbm, gains_hbm, width_hbm, out_ref,
    vis_raw, sky_raw, ids_ref, gains_ref, width_ref, vis_ref, sky_ref,
    gbuf, gat, oh, terms, snd, rbuf, slots, halo, upd, wts,
    in_sems, rs_send, rs_recv, ag_send, ag_recv, ex_send, ex_recv,
):
    blocal = ids_ref.shape[1]
    f, bl = lax.axis_index("freq"), lax.axis_index("bl")
    z, x = lax.div(bl, NX), lax.rem(bl, NX)
    own, mine = owner_of(z, x)
    not_own = jnp.logical_not(own)
    has_up, has_down = f < nf - 1, f > 0

    def peer(kz, kx):
        return lax.rem(z + kz, NZ), lax.rem(x + kx, NX)

    halo[...] = jnp.zeros_like(halo)

    barrier = pltpu.get_barrier_semaphore()
    for kz, kx in STEPS:
        tz, tx = peer(kz, kx)
        pl.semaphore_signal(barrier, inc=1, device_id=(f, tz * NX + tx), device_id_type=MESH)
    for step in (1, nf - 1):
        neighbour = lax.rem(f + step, nf)
        pl.semaphore_signal(barrier, inc=1, device_id=(neighbour, bl), device_id_type=MESH)

    loads = [
        pltpu.make_async_copy(src, dst, in_sems.at[i])
        for i, (src, dst) in enumerate(
            [
                (ids_hbm, ids_ref),
                (width_hbm, width_ref),
                (gains_hbm, gains_ref),
                (vis_hbm, vis_raw),
                (sky_hbm, sky_raw),
            ]
        )
    ]
    for load in loads:
        load.start()

    sub = lax.broadcasted_iota(jnp.int32, (8, LANE), 0)
    top = sub < CHANS

    loads[0].wait()

    def fill(i, _):
        for h in range(2):
            row = ids_ref[h : h + 1, pl.ds(pl.multiple_of(i * LANE, LANE), LANE)]
            at = pl.multiple_of(h * blocal + i * LANE, LANE)
            column = jnp.transpose(jnp.broadcast_to(row, (LANE, LANE)))
            for b in range(BLOCKS):
                station = lax.broadcasted_iota(jnp.int32, (LANE, LANE), 1) + b * LANE
                oh[b, pl.ds(at, LANE)] = jnp.where(station == column, 1.0, 0.0).astype(BF16)
        return 0

    lax.fori_loop(0, blocal // LANE, fill, 0)

    loads[1].wait()
    spread = jnp.full((8, LANE), width_ref[mine], jnp.int32).astype(F32)
    chan = jnp.bitwise_and(sub, CHANS - 1)
    taps = []
    for j in range(3 * CHANS):
        shift = j - CHANS - chan
        there = f * CHANS + (j - CHANS)
        inside = (jnp.abs(shift) <= CHANS) & (there >= 0) & (there < nf * CHANS)
        distance = shift.astype(F32)
        taps.append(
            jnp.where(inside, jnp.exp(-(distance * distance) / (2.0 * spread * spread)), 0.0)
        )
    total = functools.reduce(jnp.add, taps)
    for j in range(3 * CHANS):
        wts[j] = taps[j] / total

    loads[2].wait()
    for d in range(DIRS):
        for b in range(BLOCKS):
            lanes = slice(b * LANE, (b + 1) * LANE)
            gbuf[d, b] = jnp.concatenate(
                [gains_ref[0, d, :, lanes], gains_ref[1, d, :, lanes]], axis=0
            )

    loads[3].wait()
    for r in range(2):
        for c in range(CHANS):
            value = vis_raw[r, c].astype(F32)
            for t in range(TIMES):
                vis_ref[r, CHANS * t + c : CHANS * t + c + 1] = value[t : t + 1]
    loads[4].wait()

    def unpack(d, _):
        for r in range(2):
            for c in range(CHANS):
                value = sky_raw[d, r, c].astype(F32)
                for t in range(TIMES):
                    sky_ref[2 * d + r, CHANS * t + c : CHANS * t + c + 1] = value[t : t + 1]
        return 0

    lax.fori_loop(0, DIRS, unpack, 0)

    def swap(tile):
        return pltpu.roll(tile, CHANS, 0)

    def parts_of(tile):
        other = swap(tile)
        return jnp.where(top, tile, other), jnp.where(top, other, tile)

    def fold(a, b):
        return jnp.where(top, a, b) + swap(jnp.where(top, b, a))

    def ends(j):
        found = []
        for h in range(2):
            row = jnp.broadcast_to(ids_ref[h : h + 1, j * LANE : (j + 1) * LANE], (8, LANE))
            found.append((lax.shift_right_logical(row, 7), jnp.bitwise_and(row, LANE - 1)))
        return found

    def taken(d, blocks, at, lane, value):
        for block in blocks:
            got = jnp.take_along_axis(gbuf[d, block], lane, axis=1)
            value = got if value is None else jnp.where(at == block, got, value)
        return value

    def gather(steps, start):
        blocks = [lax.rem(x + k, NX) for k in steps]
        for j in range(blocal // LANE):
            for h, (at, lane) in enumerate(ends(j)):
                lanes = slice(h * blocal + j * LANE, h * blocal + (j + 1) * LANE)
                for d in range(DIRS):
                    rows = slice(8 * d, 8 * d + 8)
                    gat[rows, lanes] = taken(
                        d, blocks, at, lane, None if start else gat[rows, lanes]
                    )

    def chunk(j, last):
        lanes = slice(j * LANE, (j + 1) * LANE)
        after = slice(blocal + j * LANE, blocal + (j + 1) * LANE)
        (p_at, p_lane), (q_at, q_lane) = ends(j)
        sum_re, sum_im = vis_ref[0, :, lanes], vis_ref[1, :, lanes]
        kept = []
        for d in range(DIRS):
            rows = slice(8 * d, 8 * d + 8)
            l_re, l_im = parts_of(taken(d, last, p_at, p_lane, gat[rows, lanes]))
            r_re, r_im = parts_of(taken(d, last, q_at, q_lane, gat[rows, after]))
            m_re, m_im = sky_ref[2 * d, :, lanes], sky_ref[2 * d + 1, :, lanes]
            z_re = l_re * m_re - l_im * m_im
            z_im = l_re * m_im + l_im * m_re
            y_re = r_re * m_re + r_im * m_im
            y_im = r_re * m_im - r_im * m_re
            u_re = z_re * r_re + z_im * r_im
            u_im = z_im * r_re - z_re * r_im
            sum_re, sum_im = sum_re - u_re, sum_im - u_im
            kept.append((z_re, z_im, y_re, y_im, u_re, u_im))
        first, second, first_den, second_den = [], [], [], []
        for z_re, z_im, y_re, y_im, u_re, u_im in kept:
            res_re, res_im = sum_re + u_re, sum_im + u_im
            first.append(fold(res_re * y_re + res_im * y_im, res_im * y_re - res_re * y_im))
            second.append(fold(res_re * z_re + res_im * z_im, res_re * z_im - res_im * z_re))
            first_den.append(y_re * y_re + y_im * y_im)
            second_den.append(z_re * z_re + z_im * z_im)
        for d in range(0, DIRS, 2):
            first.append(fold(first_den[d], first_den[d + 1]))
            second.append(fold(second_den[d], second_den[d + 1]))
        pad = jnp.zeros((8, LANE), F32)
        terms[:, lanes] = jnp.concatenate([*first, pad], axis=0).astype(BF16)
        terms[:, after] = jnp.concatenate([*second, pad], axis=0).astype(BF16)

    def row_of(ref, e):
        return jnp.where(
            top,
            jnp.broadcast_to(ref[e : e + 1, :], (8, LANE)),
            jnp.broadcast_to(ref[CHANS + e : CHANS + e + 1, :], (8, LANE)),
        )

    def smooth(ref, side):
        return functools.reduce(
            jnp.add, [wts[side * CHANS + e] * row_of(ref, e) for e in range(CHANS)]
        )

    def finish_sends():
        @pl.when(own)
        def _():
            wait_for(slots.at[pl.ds(0, 23), pl.ds(0, 12)], rs_send)
            wait_for(slots.at[pl.ds(0, 31), pl.ds(0, 8)], ag_send)

            @pl.when(has_up)
            def _():
                wait_for(upd, ex_send.at[0])

            @pl.when(has_down)
            def _():
                wait_for(upd, ex_send.at[1])

        @pl.when(not_own)
        def _():
            wait_for(slots.at[pl.ds(0, 24), pl.ds(0, 12)], rs_send)

    def arrived(step):
        tiles = slots.at[pl.ds(0, DIRS), pl.ds(0, 8)]
        if step:
            wait_for(tiles, ag_recv.at[step])
        else:

            @pl.when(own)
            def _():
                wait_for(slots.at[pl.ds(0, DIRS - 1), pl.ds(0, 8)], ag_recv.at[0])

            @pl.when(not_own)
            def _():
                wait_for(tiles, ag_recv.at[0])

    def sweep(it, _):
        parity = lax.rem(it, 2)
        for group in ARRIVALS:

            @pl.when(it > 0)
            def _():
                for step in group:
                    arrived(step)

            if group != ARRIVALS[-1]:
                gather(group, group == ARRIVALS[0])

        @pl.when(it > 0)
        def _():
            finish_sends()

        last = [lax.rem(x + k, NX) for k in ARRIVALS[-1]]
        for j in range(blocal // LANE):
            chunk(j, last)

        for group in GROUPS:
            for kx in group:
                tx = lax.rem(x + kx, NX)
                normals = jnp.dot(terms[...], oh[tx], preferred_element_type=F32)
                for d in range(DIRS):
                    snd[d, tx, 0:8] = normals[8 * d : 8 * d + 8]
                    den = 8 * DIRS + CHANS * d
                    snd[d, tx, 8:12] = normals[den : den + CHANS]
            if group == GROUPS[0]:

                @pl.when(it == 0)
                def _():
                    pl.semaphore_wait(barrier, len(STEPS) + 2)

            for kz, kx in sorted(
                [(kz, kx) for kz in range(NZ) for kx in group if kz or kx],
                key=lambda k: -hops(*k),
            ):
                tz, tx = peer(kz, kx)
                there, which = owner_of(tz, tx)

                @pl.when(there)
                def _():
                    pltpu.make_async_remote_copy(
                        src_ref=snd.at[which, tx, pl.ds(0, 12)],
                        dst_ref=rbuf.at[kx, kz, pl.ds(0, 12)],
                        send_sem=rs_send,
                        recv_sem=rs_recv.at[kx],
                        device_id=(f, tz * NX + tx),
                        device_id_type=MESH,
                    ).start()

        @pl.when(own)
        def _():
            num, den = [snd[mine, x, 0:8]], [snd[mine, x, 8:12]]
            for kx in SUMS:
                senders = range(0 if kx else 1, NZ)
                wait_for(rbuf.at[kx, pl.ds(senders[0], len(senders)), pl.ds(0, 12)], rs_recv.at[kx])
                num.append(tree([rbuf[kx, kz, 0:8] for kz in senders]))
                den.append(tree([rbuf[kx, kz, 8:12] for kz in senders]))
            num, den = tree(num), tree(den)
            den = jnp.concatenate([den, den], axis=0)
            now = gbuf[mine, x]
            upd[...] = 0.5 * (now + (num + rho * now) / (den + rho))

            @pl.when(has_up)
            def _():
                pltpu.make_async_remote_copy(
                    src_ref=upd, dst_ref=halo.at[parity, 0],
                    send_sem=ex_send.at[0], recv_sem=ex_recv.at[parity, 0],
                    device_id=(f + 1, bl), device_id_type=MESH,
                ).start()

            @pl.when(has_down)
            def _():
                pltpu.make_async_remote_copy(
                    src_ref=upd, dst_ref=halo.at[parity, 1],
                    send_sem=ex_send.at[1], recv_sem=ex_recv.at[parity, 1],
                    device_id=(f - 1, bl), device_id_type=MESH,
                ).start()

            inner = smooth(upd, 1)

            @pl.when(has_down)
            def _():
                wait_for(halo.at[parity, 0], ex_recv.at[parity, 0])

            @pl.when(has_up)
            def _():
                wait_for(halo.at[parity, 1], ex_recv.at[parity, 1])

            gbuf[mine, x] = inner + smooth(halo.at[parity, 0], 0) + smooth(halo.at[parity, 1], 2)
            for kz, kx in sorted(STEPS, key=lambda k: (-hops(k[0], 0), -hops(0, k[1]))):
                tz, tx = peer(kz, kx)
                pltpu.make_async_remote_copy(
                    src_ref=gbuf.at[mine, x], dst_ref=gbuf.at[mine, x],
                    send_sem=ag_send, recv_sem=ag_recv.at[(NX - kx) % NX],
                    device_id=(f, tz * NX + tx), device_id_type=MESH,
                ).start()
        return 0

    lax.fori_loop(0, ITERS, sweep, 0)
    for step in range(NX):
        arrived(step)
    finish_sends()
    for d in range(DIRS):
        for b in range(BLOCKS):
            for part in range(2):
                rows = slice(CHANS * part, CHANS * part + CHANS)
                out_ref[part, d, :, b * LANE : (b + 1) * LANE] = gbuf[d, b, rows]


def body(visibilities, predicted_sky, station_pairs, start_gains, kernel_width):
    chans, stations = start_gains.shape[2:]
    blocal = station_pairs.shape[1]
    nf = lax.axis_size("freq")
    rho = float(TIMES * blocal * lax.axis_size("bl") / stations)
    hbm = pl.BlockSpec(memory_space=pltpu.HBM)
    gains = pl.pallas_call(
        functools.partial(kernel, nf, rho),
        out_shape=jax.ShapeDtypeStruct(start_gains.shape, F32),
        in_specs=[hbm] * 5,
        out_specs=pl.BlockSpec(memory_space=pltpu.VMEM),
        scratch_shapes=[
            pltpu.VMEM(visibilities.shape, BF16),
            pltpu.VMEM(predicted_sky.shape, BF16),
            pltpu.VMEM(station_pairs.shape, jnp.int32),
            pltpu.VMEM(start_gains.shape, F32),
            pltpu.SMEM(kernel_width.shape, jnp.int32),
            pltpu.VMEM((2, 8, blocal), F32),
            pltpu.VMEM((2 * DIRS, 8, blocal), F32),
            pltpu.VMEM((DIRS, BLOCKS, 8, LANE), F32),
            pltpu.VMEM((8 * DIRS, 2 * blocal), F32),
            pltpu.VMEM((BLOCKS, 2 * blocal, LANE), BF16),
            pltpu.VMEM((80, 2 * blocal), BF16),
            pltpu.VMEM((DIRS, BLOCKS, 16, LANE), F32),
            pltpu.VMEM((NX, NZ, 16, LANE), F32),
            pltpu.VMEM((NZ * NX, 16, LANE), F32),
            pltpu.VMEM((2, 2, 8, LANE), F32),
            pltpu.VMEM((8, LANE), F32),
            pltpu.VMEM((3 * CHANS, 8, LANE), F32),
            pltpu.SemaphoreType.DMA((5,)),
            pltpu.SemaphoreType.DMA,
            pltpu.SemaphoreType.DMA((NX,)),
            pltpu.SemaphoreType.DMA,
            pltpu.SemaphoreType.DMA((NX,)),
            pltpu.SemaphoreType.DMA((2,)),
            pltpu.SemaphoreType.DMA((2, 2)),
        ],
        compiler_params=pltpu.CompilerParams(
            collective_id=0, has_side_effects=True, vmem_limit_bytes=40 * 1024 * 1024
        ),
    )(*[pltpu.with_memory_space_constraint(v, pltpu.HBM) for v in (visibilities, predicted_sky, station_pairs, start_gains, kernel_width)])
    return gains


def solution(mesh):
    in_specs = (
        P(None, "freq", None, "bl"),
        P(None, None, "freq", None, "bl"),
        P(None, "bl"),
        P(None, None, "freq", None),
        P(),
    )
    out_specs = P(None, None, "freq", None)
    return jax.shard_map(body, mesh=mesh, in_specs=in_specs, out_specs=out_specs, check_vma=False)
```
